32 devices in a mesh: aux: 4 (over y, x), occ: 8 (over z, core).
Axes of the slice: x: 2, y: 2, z: 4, core: 2. Of those that a mesh axis runs over, the one named last changes fastest.
Arguments:
- amplitudes: bfloat16 [32, 512, 1024], P('aux', 'occ'), may hold values from -6 to 6
- virtual_orbitals: bfloat16 [1536, 1024], P('aux'), may hold values from -0.1875 to 0.1875
- occupied_orbitals: bfloat16 [1536, 512], P('aux'), may hold values from -0.25 to 0.25
- screening: int32 [12, 12], replicated, may hold values from 0 to 1, as said below
- pair_owner: int32 [12, 12], replicated, may hold values from 0 to 7, as said below
- pair_weight: bfloat16 [16, 128, 128], P('occ'), may hold values from 0.5 to 2
Outputs:
- owned_density: bfloat16 [32, 16, 128, 128], P('aux', 'occ')
The draws below stay inside these ranges and needn't reach their ends.
Inputs may be any that keep to these rules, and one draw needn't show every extreme that they name: `screening`: Symmetric; exactly 9 blocks (r, c) with r <= c are 1. `pair_owner`: Symmetric. Among kept blocks with r <= c, no owner holds more than 2, and some owner holds exactly 2.
All inputs are finite; a program needn't handle non-finite values.
Results may differ from the reference program's by a relative error of at most 0.0085.
Values may be sent and summed in bfloat16 or wider, within the bound.
A program may use at most 64 MiB of HBM per device.

```python
import math
import jax
import jax.numpy as jnp
from jax import lax

NOCC = 512
NVIR = 1024
NBAS = 1536
BLK = 128
MAXP = 2
NAUX = 32
NB = 12
SLOTS = 16
KEPT = 9
N_OCC = 8


def screen_plan(key):
    key_pairs = jax.random.fold_in(key, 101)
    key_owner = jax.random.fold_in(key, 202)
    key_slots = jax.random.fold_in(key, 303)
    key_rest = jax.random.fold_in(key, 404)
    count = NB * NB
    block_ids = jnp.arange(count, dtype=jnp.int32)
    first = block_ids // NB
    second = block_ids % NB
    canonical = first <= second
    shuffled = jax.random.permutation(key_pairs, count).astype(jnp.int32)
    scores = jnp.where(canonical, shuffled, count + shuffled)
    order = jnp.argsort(scores, stable=True).astype(jnp.int32)
    kept_ids = order[:KEPT]
    busiest = jax.random.randint(key_owner, (), 0, N_OCC).astype(jnp.int32)
    slot_ids = jnp.arange(SLOTS, dtype=jnp.int32)
    slot_shuffle = jax.random.permutation(key_slots, SLOTS).astype(jnp.int32)
    slot_scores = jnp.where(slot_ids // MAXP == busiest, slot_ids % MAXP - MAXP, slot_shuffle)
    slot_order = jnp.argsort(slot_scores, stable=True).astype(jnp.int32)
    kept_owners = slot_order[:KEPT] // MAXP
    base = jax.random.randint(key_rest, (count,), 0, N_OCC).astype(jnp.int32)
    owner_flat = base.at[kept_ids].set(kept_owners)
    mask_flat = jnp.zeros((count,), jnp.int32).at[kept_ids].set(1)
    upper = (first <= second).reshape(NB, NB)
    owner_grid = owner_flat.reshape(NB, NB)
    mask_grid = mask_flat.reshape(NB, NB)
    owner_grid = jnp.where(upper, owner_grid, owner_grid.T)
    mask_grid = jnp.where(upper, mask_grid, mask_grid.T)
    return (mask_grid.astype(jnp.int32), owner_grid.astype(jnp.int32))


def draw_screening(key, part):
    return screen_plan(key)[0]


def draw_pair_owner(key, part):
    return screen_plan(key)[1]


def shard_levels(key, dims, pieces, smallest, top_value):
    def one(axis_at, shards_of):
        steps = jax.random.uniform(jax.random.fold_in(jax.random.fold_in(key, 6), axis_at), (shards_of,), jnp.float32, smallest / len(pieces), top_value / len(pieces))
        return jnp.repeat(jnp.exp(steps), dims[axis_at] // shards_of).reshape((-1,) + (1,) * (len(dims) - axis_at - 1))

    level = one(*pieces[0])
    for cut in pieces[1:]:
        level = level * one(*cut)
    return level


def normal_values(rng, extent, spread, limit, pieces=(), kind=jnp.bfloat16):
    entries = jax.random.normal(rng, extent, jnp.float32) * spread
    if len(pieces) > 0:
        entries = shard_levels(rng, extent, pieces, -0.22, 0.18) * entries
    return jnp.clip(entries, min=-limit, max=limit).astype(kind)


def setup_inputs(seed: int = 0) -> dict:
    streams_of = jax.random.split(jax.random.key(seed), 7)
    amplitudes = normal_values(streams_of[0], (NAUX, NOCC, NVIR), 1.0, 6.0, ((0, 4), (1, 8)))
    virtual_orbitals = normal_values(streams_of[1], (NBAS, NVIR), NVIR ** -0.5, 0.1875, ((0, 4),))
    occupied_orbitals = normal_values(streams_of[2], (NBAS, NOCC), NOCC ** -0.5, 0.25, ((0, 4),))
    screening = draw_screening(jax.random.fold_in(streams_of[6], 71), 0)
    pair_owner = draw_pair_owner(jax.random.fold_in(streams_of[6], 71), 0)
    pair_weight = jnp.clip(jnp.exp(math.log(2.0) - 1.3862944 * jax.random.uniform(streams_of[5], (SLOTS, BLK, BLK), jnp.float32) ** shard_levels(streams_of[5], (SLOTS, BLK, BLK), ((0, 8),), -0.2, 0.2)), 0.5, 2.0).astype(jnp.bfloat16)
    return dict(amplitudes=amplitudes, virtual_orbitals=virtual_orbitals, occupied_orbitals=occupied_orbitals, screening=screening, pair_owner=pair_owner, pair_weight=pair_weight)


def slot_table(screening, pair_owner, slots):
    nblocks = screening.shape[0]
    count = nblocks * nblocks
    block_ids = jnp.arange(count, dtype=jnp.int32)
    first = block_ids // nblocks
    second = block_ids % nblocks
    keep_flag = (screening.reshape(count) == 1) & (first <= second)
    owner_flat = pair_owner.reshape(count)
    earlier = (owner_flat[:, None] == owner_flat[None, :]) & keep_flag[None, :] & (block_ids[None, :] < block_ids[:, None])
    ranks = jnp.sum(earlier.astype(jnp.int32), axis=1).astype(jnp.int32)
    target = jnp.where(keep_flag, owner_flat * MAXP + ranks, -1).astype(jnp.int32)
    matches = target[None, :] == jnp.arange(slots, dtype=jnp.int32)[:, None]
    filled = jnp.any(matches, axis=1)
    chosen = jnp.sum(jnp.where(matches, block_ids[None, :], 0), axis=1).astype(jnp.int32)
    return filled, chosen // nblocks, chosen % nblocks


def reference(amplitudes, virtual_orbitals, occupied_orbitals, screening, pair_owner, pair_weight):
    filled, row_blocks, col_blocks = slot_table(screening, pair_owner, MAXP * N_OCC)
    weights = pair_weight.astype(jnp.float32)

    def one_function(amplitude):
        half = jnp.dot(amplitude, virtual_orbitals.T, preferred_element_type=jnp.float32).astype(jnp.bfloat16)
        full = jnp.dot(occupied_orbitals, half, preferred_element_type=jnp.float32).astype(jnp.bfloat16)
        nblocks = screening.shape[0]
        grid = full.reshape(nblocks, BLK, nblocks, BLK)
        direct = grid[row_blocks, :, col_blocks, :]
        mirror = grid[col_blocks, :, row_blocks, :]
        folded = (direct.astype(jnp.float32) + jnp.swapaxes(mirror, -1, -2).astype(jnp.float32)).astype(jnp.bfloat16)
        folded = jnp.where(filled[:, None, None], folded, jnp.zeros_like(folded))
        return (weights * folded.astype(jnp.float32)).astype(jnp.bfloat16)

    return lax.map(one_function, amplitudes)
```

```python
import functools

import jax
import jax.numpy as jnp
from jax import lax
from jax.experimental import pallas as pl
from jax.experimental.pallas import tpu as pltpu
from jax.sharding import PartitionSpec as P

MAXP = 2
MESH = pl.DeviceIdType.MESH


def slot_table(screening, pair_owner, slots):
    nblocks = screening.shape[0]
    count = nblocks * nblocks
    block_ids = jnp.arange(count, dtype=jnp.int32)
    first = block_ids // nblocks
    second = block_ids % nblocks
    keep_flag = (screening.reshape(count) == 1) & (first <= second)
    owner_flat = pair_owner.reshape(count)
    earlier = (
        (owner_flat[:, None] == owner_flat[None, :])
        & keep_flag[None, :]
        & (block_ids[None, :] < block_ids[:, None])
    )
    ranks = jnp.sum(earlier.astype(jnp.int32), axis=1)
    target = jnp.where(keep_flag, owner_flat * MAXP + ranks, -1)
    matches = target[None, :] == jnp.arange(slots, dtype=jnp.int32)[:, None]
    filled = jnp.any(matches, axis=1)
    chosen = jnp.sum(jnp.where(matches, block_ids[None, :], 0), axis=1)
    return filled, chosen // nblocks, chosen % nblocks


def fused(
    groups, peers,
    row_blocks, col_blocks, amp, virt, occ, out,
    moved, virt_all, occ_all, half, fold,
    x_send, x_recv, g_send, g_recv, s_send, s_recv, f_send, f_recv, local,
):
    aux = lax.axis_index("aux")
    me = lax.axis_index("occ")
    core = lax.rem(me, 2)
    sibling = me + 1 - 2 * core
    own = moved.shape[1]
    inner = moved.shape[2]
    rows = virt.shape[0]
    part = rows // 2
    width = half.shape[2]
    per_shard = rows // width

    def away(j):
        return lax.rem(me + j, peers)

    def other(j):
        return lax.rem(aux + j, groups)

    barrier = pltpu.get_barrier_semaphore()

    def greet(j, carry):
        pl.semaphore_signal(barrier, inc=1, device_id={"occ": away(j)}, device_id_type=MESH)
        return carry

    lax.fori_loop(1, peers, greet, 0)
    for j in range(1, groups):
        pl.semaphore_signal(barrier, inc=1, device_id={"aux": other(j)}, device_id_type=MESH)

    keep = [
        pltpu.make_async_copy(virt, virt_all.at[pl.ds(pl.multiple_of(aux * rows, rows), rows)], local.at[0]),
        pltpu.make_async_copy(occ, occ_all.at[pl.ds(aux * per_shard, per_shard)], local.at[1]),
        pltpu.make_async_copy(amp.at[pl.ds(me * own, own)], moved.at[me], local.at[2]),
    ]
    for copy in keep:
        copy.start()
    pl.semaphore_wait(barrier, peers - 1 + groups - 1)

    def x_copy(j):
        to = away(j)
        return pltpu.make_async_remote_copy(
            src_ref=amp.at[pl.ds(to * own, own)],
            dst_ref=moved.at[me],
            send_sem=x_send.at[j - 1],
            recv_sem=x_recv.at[j - 1],
            device_id={"occ": to},
            device_id_type=MESH,
        )

    def halves(which, shard):
        if which:
            rows_of = pl.ds(pl.multiple_of(core * (width // 2), width // 2), width // 2)
            return occ_all.at[pl.ds(shard * per_shard, per_shard), rows_of]
        return virt_all.at[pl.ds(pl.multiple_of(shard * rows + core * part, part), part)]

    def g_copy(j, which):
        if which:
            rows_of = pl.ds(pl.multiple_of(core * (width // 2), width // 2), width // 2)
            src = occ.at[:, rows_of]
        else:
            src = virt.at[pl.ds(pl.multiple_of(core * part, part), part)]
        return pltpu.make_async_remote_copy(
            src_ref=src,
            dst_ref=halves(which, aux),
            send_sem=g_send.at[which, j - 1],
            recv_sem=g_recv.at[which, j - 1],
            device_id={"aux": other(j)},
            device_id_type=MESH,
        )

    def s_copy(j, which):
        place = halves(which, lax.rem(aux + groups - j, groups))
        return pltpu.make_async_remote_copy(
            src_ref=place,
            dst_ref=place,
            send_sem=s_send.at[which, j - 1],
            recv_sem=s_recv.at[which, j - 1],
            device_id={"occ": sibling},
            device_id_type=MESH,
        )

    def f_copy(j):
        to = away(j)
        return pltpu.make_async_remote_copy(
            src_ref=fold.at[to],
            dst_ref=out.at[pl.ds(me * own, own)],
            send_sem=f_send.at[j - 1],
            recv_sem=f_recv.at[j - 1],
            device_id={"occ": to},
            device_id_type=MESH,
        )

    def each(action, first=1, last=None):
        def step(j, carry):
            action(j)
            return carry

        lax.fori_loop(first, peers if last is None else last, step, 0)

    for which in range(2):
        for j in range(1, groups):
            g_copy(j, which).start()
    each(lambda j: x_copy(j).start())

    for which in range(2):
        for j in range(1, groups):
            g_copy(j, which).wait_recv()
            s_copy(j, which).start()
    for copy in keep:
        copy.wait()
    for which in range(2):
        for j in range(1, groups):
            s_copy(j, which).wait_recv()
    each(lambda j: x_copy(j).wait_recv())

    for p in range(own):
        def project(g, carry):
            x = moved[:, p]
            if inner % 16:
                x = x.astype(jnp.float32)
            x = x.reshape(peers * inner, x.shape[-1]).astype(jnp.bfloat16)
            v = virt_all[pl.ds(pl.multiple_of(g * rows, rows), rows), :]
            h = lax.dot_general(
                x, v, (((1,), (1,)), ((), ())), preferred_element_type=jnp.float32
            ).astype(jnp.bfloat16)
            for t in range(per_shard):
                half[g * per_shard + t] = h[:, t * width : (t + 1) * width]
            return carry

        lax.fori_loop(0, groups, project, 0)

        def block(r, c):
            return (
                jnp.dot(occ_all[r], half[c], preferred_element_type=jnp.float32)
                .astype(jnp.bfloat16)
                .astype(jnp.float32)
            )

        def make(j):
            to = away(j)
            for s in range(MAXP):
                r = row_blocks[to * MAXP + s]
                c = col_blocks[to * MAXP + s]
                both = block(r, c) + block(c, r).T
                fold[to, p, s] = both.astype(jnp.bfloat16)

        if p < own - 1:
            each(make, 0)

    def finish(j):
        make(j)
        f_copy(j).start()

    each(finish)
    make(0)
    mine = pltpu.make_async_copy(fold.at[me], out.at[pl.ds(me * own, own)], local.at[3])
    mine.start()

    for which in range(2):
        for j in range(1, groups):
            g_copy(j, which).wait_send()
            s_copy(j, which).wait_send()
    each(lambda j: x_copy(j).wait_send())
    each(lambda j: f_copy(j).wait_recv())
    each(lambda j: f_copy(j).wait_send())
    mine.wait()


def per_device(groups, peers, amplitudes, virtual_orbitals, occupied_orbitals, screening, pair_owner, pair_weight):
    group_size, inner, virtual_count = amplitudes.shape
    rows = virtual_orbitals.shape[0]
    occupied_count = occupied_orbitals.shape[1]
    own = group_size // peers
    nblocks = screening.shape[0]
    width = pair_weight.shape[1]
    filled, row_blocks, col_blocks = slot_table(screening, pair_owner, peers * MAXP)
    kind = jnp.bfloat16
    dma = pltpu.SemaphoreType.DMA
    folded = pl.pallas_call(
        functools.partial(fused, groups, peers),
        out_shape=jax.ShapeDtypeStruct((group_size, MAXP, width, width), kind),
        in_specs=[pl.BlockSpec(memory_space=pltpu.SMEM)] * 2 + [pl.BlockSpec(memory_space=pl.ANY)] * 3,
        out_specs=pl.BlockSpec(memory_space=pl.ANY),
        scratch_shapes=[
            pltpu.VMEM((peers, own, inner, virtual_count), kind),
            pltpu.VMEM((groups * rows, virtual_count), kind),
            pltpu.VMEM((nblocks, width, occupied_count), kind),
            pltpu.VMEM((nblocks, occupied_count, width), kind),
            pltpu.VMEM((peers, own, MAXP, width, width), kind),
            dma((peers - 1,)),
            dma((peers - 1,)),
            dma((2, groups - 1)),
            dma((2, groups - 1)),
            dma((2, groups - 1)),
            dma((2, groups - 1)),
            dma((peers - 1,)),
            dma((peers - 1,)),
            dma((4,)),
        ],
        compiler_params=pltpu.CompilerParams(
            collective_id=0, has_side_effects=True, vmem_limit_bytes=40 * 1024 * 1024
        ),
    )(
        row_blocks,
        col_blocks,
        amplitudes,
        virtual_orbitals,
        occupied_orbitals.reshape(rows // width, width, occupied_count),
    )
    mine = lax.dynamic_slice_in_dim(filled, lax.axis_index("occ") * MAXP, MAXP)
    weighted = pair_weight.astype(jnp.float32)[None] * folded.astype(jnp.float32)
    return jnp.where(mine[None, :, None, None], weighted, 0.0).astype(jnp.bfloat16)


def solution(mesh):
    return jax.shard_map(
        functools.partial(per_device, mesh.shape["aux"], mesh.shape["occ"]),
        mesh=mesh,
        in_specs=(
            P("aux", "occ", None),
            P("aux", None),
            P("aux", None),
            P(),
            P(),
            P("occ", None, None),
        ),
        out_specs=P("aux", "occ", None, None),
        check_vma=False,
    )
```

```python
import functools

import jax
import jax.numpy as jnp
from jax import lax
from jax.experimental import pallas as pl
from jax.experimental.pallas import tpu as pltpu
from jax.sharding import PartitionSpec as P

MAXP = 2
MESH = pl.DeviceIdType.MESH


def slot_table(screening, pair_owner, slots):
    nblocks = screening.shape[0]
    count = nblocks * nblocks
    block_ids = jnp.arange(count, dtype=jnp.int32)
    first = block_ids // nblocks
    second = block_ids % nblocks
    keep_flag = (screening.reshape(count) == 1) & (first <= second)
    owner_flat = pair_owner.reshape(count)
    earlier = (
        (owner_flat[:, None] == owner_flat[None, :])
        & keep_flag[None, :]
        & (block_ids[None, :] < block_ids[:, None])
    )
    ranks = jnp.sum(earlier.astype(jnp.int32), axis=1)
    target = jnp.where(keep_flag, owner_flat * MAXP + ranks, -1)
    matches = target[None, :] == jnp.arange(slots, dtype=jnp.int32)[:, None]
    filled = jnp.any(matches, axis=1)
    chosen = jnp.sum(jnp.where(matches, block_ids[None, :], 0), axis=1)
    return filled, chosen // nblocks, chosen % nblocks


def fused(
    groups, peers,
    row_blocks, col_blocks, amp, virt, occ, out,
    moved, virt_all, occ_all, half, fold,
    x_send, x_recv, n_send, n_recv, d_send, d_recv, s_send, s_recv, f_send, f_recv, local,
):
    aux = lax.axis_index("aux")
    me = lax.axis_index("occ")
    core = lax.rem(me, 2)
    sibling = me + 1 - 2 * core
    own = moved.shape[1]
    inner = moved.shape[2]
    rows = virt.shape[0]
    half_group = peers // 2
    width = half.shape[3]
    per_shard = rows // width

    def away(j):
        return lax.rem(me + j, peers)

    beside = aux + 1 - 2 * lax.rem(aux, 2)
    across = lax.rem(aux + 2, groups)
    corner = lax.rem(beside + 2, groups)

    barrier = pltpu.get_barrier_semaphore()

    def greet(j, carry):
        pl.semaphore_signal(barrier, inc=1, device_id={"occ": away(j)}, device_id_type=MESH)
        return carry

    lax.fori_loop(1, peers, greet, 0)
    for near in (beside, across):
        pl.semaphore_signal(barrier, inc=1, device_id={"aux": near}, device_id_type=MESH)

    keep = [
        pltpu.make_async_copy(virt, virt_all.at[pl.ds(pl.multiple_of(aux * rows, rows), rows)], local.at[0]),
        pltpu.make_async_copy(occ, occ_all.at[pl.ds(aux * per_shard, per_shard)], local.at[1]),
        pltpu.make_async_copy(amp.at[pl.ds(me * own, own)], moved.at[me], local.at[2]),
    ]
    for copy in keep:
        copy.start()
    pl.semaphore_wait(barrier, peers + 1)

    def x_copy(j):
        to = away(j)
        return pltpu.make_async_remote_copy(
            src_ref=amp.at[pl.ds(to * own, own)],
            dst_ref=moved.at[me],
            send_sem=x_send.at[j - 1],
            recv_sem=x_recv.at[j - 1],
            device_id={"occ": to},
            device_id_type=MESH,
        )

    def piece(which, shard, first, count):
        if which:
            quarter = width // 4
            rows_of = pl.ds(pl.multiple_of(first * quarter, quarter), count * quarter)
            return occ_all.at[pl.ds(shard * per_shard, per_shard), rows_of]
        quarter = rows // 4
        return virt_all.at[pl.ds(pl.multiple_of(shard * rows + first * quarter, quarter), count * quarter)]

    def n_copy(which, way, q):
        first = 2 * core + q
        if which:
            quarter = width // 4
            src = occ.at[:, pl.ds(pl.multiple_of(first * quarter, quarter), quarter)]
        else:
            quarter = rows // 4
            src = virt.at[pl.ds(pl.multiple_of(first * quarter, quarter), quarter)]
        return pltpu.make_async_remote_copy(
            src_ref=src,
            dst_ref=piece(which, aux, first, 1),
            send_sem=n_send.at[which, way, q],
            recv_sem=n_recv.at[which, way, q],
            device_id={"aux": (beside, across)[way]},
            device_id_type=MESH,
        )

    def d_copy(which, q):
        place = piece(which, (beside, across)[q], 2 * core + q, 1)
        return pltpu.make_async_remote_copy(
            src_ref=place,
            dst_ref=place,
            send_sem=d_send.at[which, q],
            recv_sem=d_recv.at[which, q],
            device_id={"aux": (across, beside)[q]},
            device_id_type=MESH,
        )

    def s_copy(which, j):
        place = piece(which, (beside, across, corner)[j], 2 * core, 2)
        return pltpu.make_async_remote_copy(
            src_ref=place,
            dst_ref=place,
            send_sem=s_send.at[which, j],
            recv_sem=s_recv.at[which, j],
            device_id={"occ": sibling},
            device_id_type=MESH,
        )

    def f_copy(j):
        to = away(j)
        return pltpu.make_async_remote_copy(
            src_ref=fold.at[to],
            dst_ref=out.at[pl.ds(me * own, own)],
            send_sem=f_send.at[j - 1],
            recv_sem=f_recv.at[j - 1],
            device_id={"occ": to},
            device_id_type=MESH,
        )

    def each(action):
        def step(t, carry):
            action(half_group + (t + 1) // 2 * (2 * lax.rem(t, 2) - 1))
            return carry

        lax.fori_loop(0, peers - 1, step, 0)

    for late in range(2):
        for which in range(2):
            for way in range(2):
                n_copy(which, way, (way + late) % 2).start()
    each(lambda j: x_copy(j).start())

    for which in range(2):
        for way in range(2):
            n_copy(which, way, way).wait_recv()
            d_copy(which, way).start()
    for which in range(2):
        for way in range(2):
            n_copy(which, way, 1 - way).wait_recv()
            s_copy(which, way).start()
    for which in range(2):
        for q in range(2):
            d_copy(which, q).wait_recv()
        s_copy(which, 2).start()
    for copy in keep:
        copy.wait()
    for which in range(2):
        for j in range(3):
            s_copy(which, j).wait_recv()

    base = me // half_group * half_group

    def arrived(source):
        x_copy(lax.rem(me - source + peers, peers)).wait_recv()

    def project(p, start):
        def step(g, carry):
            x = moved[pl.ds(start, half_group), p]
            if inner % 16:
                x = x.astype(jnp.float32)
            count = half_group * inner
            x = x.reshape(count, x.shape[-1]).astype(jnp.bfloat16)
            v = virt_all[pl.ds(pl.multiple_of(g * rows, rows), rows), :]
            h = lax.dot_general(
                x, v, (((1,), (1,)), ((), ())), preferred_element_type=jnp.float32
            ).astype(jnp.bfloat16)
            place = pl.ds(pl.multiple_of(start * inner, count), count)
            for t in range(per_shard):
                half[p, g * per_shard + t, place, :] = h[:, t * width : (t + 1) * width]
            return carry

        lax.fori_loop(0, groups, step, 0)

    def near(t, carry):
        arrived(base + lax.rem(me - base + t, half_group))
        return carry

    def far(t, carry):
        arrived(half_group - base + t)
        return carry

    lax.fori_loop(1, half_group, near, 0)
    for p in range(own):
        project(p, base)
    lax.fori_loop(0, half_group, far, 0)
    for p in range(own):
        project(p, half_group - base)

    def block(p, r, c):
        return (
            jnp.dot(occ_all[r], half[p, c], preferred_element_type=jnp.float32)
            .astype(jnp.bfloat16)
            .astype(jnp.float32)
        )

    def make(j):
        to = away(j)
        for p in range(own):
            for s in range(MAXP):
                r = row_blocks[to * MAXP + s]
                c = col_blocks[to * MAXP + s]
                both = block(p, r, c) + block(p, c, r).T
                fold[to, p, s] = both.astype(jnp.bfloat16)

    def finish(j):
        make(j)
        f_copy(j).start()

    each(finish)
    make(0)
    mine = pltpu.make_async_copy(fold.at[me], out.at[pl.ds(me * own, own)], local.at[3])
    mine.start()

    for which in range(2):
        for way in range(2):
            for q in range(2):
                n_copy(which, way, q).wait_send()
            d_copy(which, way).wait_send()
        for j in range(3):
            s_copy(which, j).wait_send()
    each(lambda j: x_copy(j).wait_send())
    each(lambda j: f_copy(j).wait_recv())
    each(lambda j: f_copy(j).wait_send())
    mine.wait()


def per_device(groups, peers, amplitudes, virtual_orbitals, occupied_orbitals, screening, pair_owner, pair_weight):
    group_size, inner, virtual_count = amplitudes.shape
    rows = virtual_orbitals.shape[0]
    occupied_count = occupied_orbitals.shape[1]
    own = group_size // peers
    nblocks = screening.shape[0]
    width = pair_weight.shape[1]
    filled, row_blocks, col_blocks = slot_table(screening, pair_owner, peers * MAXP)
    kind = jnp.bfloat16
    dma = pltpu.SemaphoreType.DMA
    folded = pl.pallas_call(
        functools.partial(fused, groups, peers),
        out_shape=jax.ShapeDtypeStruct((group_size, MAXP, width, width), kind),
        in_specs=[pl.BlockSpec(memory_space=pltpu.SMEM)] * 2 + [pl.BlockSpec(memory_space=pl.ANY)] * 3,
        out_specs=pl.BlockSpec(memory_space=pl.ANY),
        scratch_shapes=[
            pltpu.VMEM((peers, own, inner, virtual_count), kind),
            pltpu.VMEM((groups * rows, virtual_count), kind),
            pltpu.VMEM((nblocks, width, occupied_count), kind),
            pltpu.VMEM((own, nblocks, occupied_count, width), kind),
            pltpu.VMEM((peers, own, MAXP, width, width), kind),
            dma((peers - 1,)),
            dma((peers - 1,)),
            dma((2, 2, 2)),
            dma((2, 2, 2)),
            dma((2, 2)),
            dma((2, 2)),
            dma((2, 3)),
            dma((2, 3)),
            dma((peers - 1,)),
            dma((peers - 1,)),
            dma((4,)),
        ],
        compiler_params=pltpu.CompilerParams(
            collective_id=0, has_side_effects=True, vmem_limit_bytes=60 * 1024 * 1024
        ),
    )(
        row_blocks,
        col_blocks,
        amplitudes,
        virtual_orbitals,
        occupied_orbitals.reshape(rows // width, width, occupied_count),
    )
    mine = lax.dynamic_slice_in_dim(filled, lax.axis_index("occ") * MAXP, MAXP)
    weighted = pair_weight.astype(jnp.float32)[None] * folded.astype(jnp.float32)
    return jnp.where(mine[None, :, None, None], weighted, 0.0).astype(jnp.bfloat16)


def solution(mesh):
    return jax.shard_map(
        functools.partial(per_device, mesh.shape["aux"], mesh.shape["occ"]),
        mesh=mesh,
        in_specs=(
            P("aux", "occ", None),
            P("aux", None),
            P("aux", None),
            P(),
            P(),
            P("occ", None, None),
        ),
        out_specs=P("aux", "occ", None, None),
        check_vma=False,
    )
```

```python
import functools

import jax
import jax.numpy as jnp
from jax import lax
from jax.experimental import pallas as pl
from jax.experimental.pallas import tpu as pltpu
from jax.sharding import PartitionSpec as P

MAXP = 2
MESH = pl.DeviceIdType.MESH


def slot_table(screening, pair_owner, slots):
    nblocks = screening.shape[0]
    count = nblocks * nblocks
    block_ids = jnp.arange(count, dtype=jnp.int32)
    first = block_ids // nblocks
    second = block_ids % nblocks
    keep_flag = (screening.reshape(count) == 1) & (first <= second)
    owner_flat = pair_owner.reshape(count)
    earlier = (
        (owner_flat[:, None] == owner_flat[None, :])
        & keep_flag[None, :]
        & (block_ids[None, :] < block_ids[:, None])
    )
    ranks = jnp.sum(earlier.astype(jnp.int32), axis=1)
    target = jnp.where(keep_flag, owner_flat * MAXP + ranks, -1)
    matches = target[None, :] == jnp.arange(slots, dtype=jnp.int32)[:, None]
    filled = jnp.any(matches, axis=1)
    chosen = jnp.sum(jnp.where(matches, block_ids[None, :], 0), axis=1)
    return filled, chosen // nblocks, chosen % nblocks


def fused(
    groups, peers,
    row_blocks, col_blocks, amp, virt, occ, out,
    moved, virt_all, occ_all, half, fold,
    x_send, x_recv, n_send, n_recv, d_send, d_recv, s_send, s_recv, f_send, f_recv, local,
):
    aux = lax.axis_index("aux")
    me = lax.axis_index("occ")
    core = lax.rem(me, 2)
    sibling = me + 1 - 2 * core
    own = moved.shape[1]
    inner = moved.shape[2]
    rows = virt.shape[0]
    half_group = peers // 2
    width = half.shape[3]
    per_shard = rows // width

    def away(j):
        return lax.rem(me + j, peers)

    beside = aux + 1 - 2 * lax.rem(aux, 2)
    across = lax.rem(aux + 2, groups)
    corner = lax.rem(beside + 2, groups)

    barrier = pltpu.get_barrier_semaphore()

    def greet(j, carry):
        pl.semaphore_signal(barrier, inc=1, device_id={"occ": away(j)}, device_id_type=MESH)
        return carry

    lax.fori_loop(1, peers, greet, 0)
    for near in (beside, across):
        pl.semaphore_signal(barrier, inc=1, device_id={"aux": near}, device_id_type=MESH)

    keep = [
        pltpu.make_async_copy(virt, virt_all.at[pl.ds(pl.multiple_of(aux * rows, rows), rows)], local.at[0]),
        pltpu.make_async_copy(occ, occ_all.at[pl.ds(aux * per_shard, per_shard)], local.at[1]),
        pltpu.make_async_copy(amp.at[pl.ds(me * own, own)], moved.at[me], local.at[2]),
    ]
    for copy in keep:
        copy.start()
    pl.semaphore_wait(barrier, peers + 1)

    def x_copy(j):
        to = away(j)
        return pltpu.make_async_remote_copy(
            src_ref=amp.at[pl.ds(to * own, own)],
            dst_ref=moved.at[me],
            send_sem=x_send.at[j - 1],
            recv_sem=x_recv.at[j - 1],
            device_id={"occ": to},
            device_id_type=MESH,
        )

    def piece(which, shard, first, count):
        if which:
            quarter = width // 4
            rows_of = pl.ds(pl.multiple_of(first * quarter, quarter), count * quarter)
            return occ_all.at[pl.ds(shard * per_shard, per_shard), rows_of]
        quarter = rows // 4
        return virt_all.at[pl.ds(pl.multiple_of(shard * rows + first * quarter, quarter), count * quarter)]

    def n_copy(which, way, q):
        first = 2 * core + q
        if which:
            quarter = width // 4
            src = occ.at[:, pl.ds(pl.multiple_of(first * quarter, quarter), quarter)]
        else:
            quarter = rows // 4
            src = virt.at[pl.ds(pl.multiple_of(first * quarter, quarter), quarter)]
        return pltpu.make_async_remote_copy(
            src_ref=src,
            dst_ref=piece(which, aux, first, 1),
            send_sem=n_send.at[which, way, q],
            recv_sem=n_recv.at[which, way, q],
            device_id={"aux": (beside, across)[way]},
            device_id_type=MESH,
        )

    def d_copy(which, q):
        place = piece(which, (beside, across)[q], 2 * core + q, 1)
        return pltpu.make_async_remote_copy(
            src_ref=place,
            dst_ref=place,
            send_sem=d_send.at[which, q],
            recv_sem=d_recv.at[which, q],
            device_id={"aux": (across, beside)[q]},
            device_id_type=MESH,
        )

    def s_copy(which, j):
        place = piece(which, (beside, across, corner)[j], 2 * core, 2)
        return pltpu.make_async_remote_copy(
            src_ref=place,
            dst_ref=place,
            send_sem=s_send.at[which, j],
            recv_sem=s_recv.at[which, j],
            device_id={"occ": sibling},
            device_id_type=MESH,
        )

    def f_copy(j):
        to = away(j)
        return pltpu.make_async_remote_copy(
            src_ref=fold.at[to],
            dst_ref=out.at[pl.ds(me * own, own)],
            send_sem=f_send.at[j - 1],
            recv_sem=f_recv.at[j - 1],
            device_id={"occ": to},
            device_id_type=MESH,
        )

    def each(action):
        def step(t, carry):
            action(half_group + (t + 1) // 2 * (2 * lax.rem(t, 2) - 1))
            return carry

        lax.fori_loop(0, peers - 1, step, 0)

    def spread(which):
        for late in range(2):
            for way in range(2):
                n_copy(which, way, (way + late) % 2).start()

    def pass_on(which):
        for way in range(2):
            n_copy(which, way, way).wait_recv()
            d_copy(which, way).start()

    def share_sides(which):
        for way in range(2):
            n_copy(which, way, 1 - way).wait_recv()
            s_copy(which, way).start()

    def share_corner(which):
        for q in range(2):
            d_copy(which, q).wait_recv()
        s_copy(which, 2).start()

    spread(0)
    each(lambda j: x_copy(j).start())
    pass_on(0)
    spread(1)
    share_sides(0)
    share_corner(0)
    pass_on(1)
    share_sides(1)
    for copy in keep:
        copy.wait()
    for j in range(3):
        s_copy(0, j).wait_recv()

    base = me // half_group * half_group

    def arrived(source):
        x_copy(lax.rem(me - source + peers, peers)).wait_recv()

    def project(p, start):
        def step(g, carry):
            x = moved[pl.ds(start, half_group), p]
            if inner % 16:
                x = x.astype(jnp.float32)
            count = half_group * inner
            x = x.reshape(count, x.shape[-1]).astype(jnp.bfloat16)
            v = virt_all[pl.ds(pl.multiple_of(g * rows, rows), rows), :]
            h = lax.dot_general(
                x, v, (((1,), (1,)), ((), ())), preferred_element_type=jnp.float32
            ).astype(jnp.bfloat16)
            place = pl.ds(pl.multiple_of(start * inner, count), count)
            for t in range(per_shard):
                half[p, g * per_shard + t, place, :] = h[:, t * width : (t + 1) * width]
            return carry

        lax.fori_loop(0, groups, step, 0)

    def near(t, carry):
        arrived(base + lax.rem(me - base + t, half_group))
        return carry

    def far(t, carry):
        arrived(half_group - base + t)
        return carry

    lax.fori_loop(1, half_group, near, 0)
    for p in range(own):
        project(p, base)
    share_corner(1)
    lax.fori_loop(0, half_group, far, 0)
    for p in range(own):
        project(p, half_group - base)

    for j in range(3):
        s_copy(1, j).wait_recv()

    def block(p, r, c):
        return (
            jnp.dot(occ_all[r], half[p, c], preferred_element_type=jnp.float32)
            .astype(jnp.bfloat16)
            .astype(jnp.float32)
        )

    def make(j):
        to = away(j)
        for p in range(own):
            for s in range(MAXP):
                r = row_blocks[to * MAXP + s]
                c = col_blocks[to * MAXP + s]
                both = block(p, r, c) + block(p, c, r).T
                fold[to, p, s] = both.astype(jnp.bfloat16)

    def finish(j):
        make(j)
        f_copy(j).start()

    each(finish)
    make(0)
    mine = pltpu.make_async_copy(fold.at[me], out.at[pl.ds(me * own, own)], local.at[3])
    mine.start()

    for which in range(2):
        for way in range(2):
            for q in range(2):
                n_copy(which, way, q).wait_send()
            d_copy(which, way).wait_send()
        for j in range(3):
            s_copy(which, j).wait_send()
    each(lambda j: x_copy(j).wait_send())
    each(lambda j: f_copy(j).wait_recv())
    each(lambda j: f_copy(j).wait_send())
    mine.wait()


def per_device(groups, peers, amplitudes, virtual_orbitals, occupied_orbitals, screening, pair_owner, pair_weight):
    group_size, inner, virtual_count = amplitudes.shape
    rows = virtual_orbitals.shape[0]
    occupied_count = occupied_orbitals.shape[1]
    own = group_size // peers
    nblocks = screening.shape[0]
    width = pair_weight.shape[1]
    filled, row_blocks, col_blocks = slot_table(screening, pair_owner, peers * MAXP)
    kind = jnp.bfloat16
    dma = pltpu.SemaphoreType.DMA
    folded = pl.pallas_call(
        functools.partial(fused, groups, peers),
        out_shape=jax.ShapeDtypeStruct((group_size, MAXP, width, width), kind),
        in_specs=[pl.BlockSpec(memory_space=pltpu.SMEM)] * 2 + [pl.BlockSpec(memory_space=pl.ANY)] * 3,
        out_specs=pl.BlockSpec(memory_space=pl.ANY),
        scratch_shapes=[
            pltpu.VMEM((peers, own, inner, virtual_count), kind),
            pltpu.VMEM((groups * rows, virtual_count), kind),
            pltpu.VMEM((nblocks, width, occupied_count), kind),
            pltpu.VMEM((own, nblocks, occupied_count, width), kind),
            pltpu.VMEM((peers, own, MAXP, width, width), kind),
            dma((peers - 1,)),
            dma((peers - 1,)),
            dma((2, 2, 2)),
            dma((2, 2, 2)),
            dma((2, 2)),
            dma((2, 2)),
            dma((2, 3)),
            dma((2, 3)),
            dma((peers - 1,)),
            dma((peers - 1,)),
            dma((4,)),
        ],
        compiler_params=pltpu.CompilerParams(
            collective_id=0, has_side_effects=True, vmem_limit_bytes=60 * 1024 * 1024
        ),
    )(
        row_blocks,
        col_blocks,
        amplitudes,
        virtual_orbitals,
        occupied_orbitals.reshape(rows // width, width, occupied_count),
    )
    mine = lax.dynamic_slice_in_dim(filled, lax.axis_index("occ") * MAXP, MAXP)
    weighted = pair_weight.astype(jnp.float32)[None] * folded.astype(jnp.float32)
    return jnp.where(mine[None, :, None, None], weighted, 0.0).astype(jnp.bfloat16)


def solution(mesh):
    return jax.shard_map(
        functools.partial(per_device, mesh.shape["aux"], mesh.shape["occ"]),
        mesh=mesh,
        in_specs=(
            P("aux", "occ", None),
            P("aux", None),
            P("aux", None),
            P(),
            P(),
            P("occ", None, None),
        ),
        out_specs=P("aux", "occ", None, None),
        check_vma=False,
    )
```

```python
import functools

import jax
import jax.numpy as jnp
from jax import lax
from jax.experimental import pallas as pl
from jax.experimental.pallas import tpu as pltpu
from jax.sharding import PartitionSpec as P

MAXP = 2
MESH = pl.DeviceIdType.MESH


def slot_table(screening, pair_owner, nblocks, lanes):
    lane = lax.broadcasted_iota(jnp.int32, (1, lanes), 1)
    owner, rank = lane // MAXP, lane % MAXP

    def row(r, carry):
        def column(c, carry):
            rows, columns, filled, count = carry
            kept = (owner == pair_owner[r, c]) & (jnp.full_like(lane, screening[r, c]) == 1)
            here = kept & (rank == count)
            return (
                jnp.where(here, r, rows),
                jnp.where(here, c, columns),
                jnp.where(here, 1, filled),
                jnp.where(kept, count + 1, count),
            )

        return lax.fori_loop(r, nblocks, column, carry)

    none = jnp.zeros_like(lane)
    return lax.fori_loop(0, nblocks, row, (none,) * 4)[:3]


def fused(
    groups, peers,
    screening, pair_owner, amp, virt, occ, out,
    moved, virt_all, occ_all, half, fold, lines, table,
    x_send, x_recv, n_send, n_recv, d_send, d_recv, s_send, s_recv, f_send, f_recv, local,
):
    aux = lax.axis_index("aux")
    me = lax.axis_index("occ")
    core = lax.rem(me, 2)
    sibling = me + 1 - 2 * core
    own = moved.shape[1]
    inner = moved.shape[2]
    rows = virt.shape[0]
    half_group = peers // 2
    width = half.shape[3]
    per_shard = rows // width

    def away(j):
        return lax.rem(me + j, peers)

    beside = aux + 1 - 2 * lax.rem(aux, 2)
    across = lax.rem(aux + 2, groups)
    corner = lax.rem(beside + 2, groups)

    barrier = pltpu.get_barrier_semaphore()

    def greet(j, carry):
        pl.semaphore_signal(barrier, inc=1, device_id={"occ": away(j)}, device_id_type=MESH)
        return carry

    lax.fori_loop(1, peers, greet, 0)
    for near in (beside, across):
        pl.semaphore_signal(barrier, inc=1, device_id={"aux": near}, device_id_type=MESH)

    keep = [
        pltpu.make_async_copy(virt, virt_all.at[pl.ds(pl.multiple_of(aux * rows, rows), rows)], local.at[0]),
        pltpu.make_async_copy(occ, occ_all.at[pl.ds(aux * per_shard, per_shard)], local.at[1]),
        pltpu.make_async_copy(amp.at[pl.ds(me * own, own)], moved.at[me], local.at[2]),
    ]
    for copy in keep:
        copy.start()
    pl.semaphore_wait(barrier, peers + 1)

    def x_copy(j):
        to = away(j)
        return pltpu.make_async_remote_copy(
            src_ref=amp.at[pl.ds(to * own, own)],
            dst_ref=moved.at[me],
            send_sem=x_send.at[j - 1],
            recv_sem=x_recv.at[j - 1],
            device_id={"occ": to},
            device_id_type=MESH,
        )

    def piece(which, shard, first, count):
        if which:
            quarter = width // 4
            rows_of = pl.ds(pl.multiple_of(first * quarter, quarter), count * quarter)
            return occ_all.at[pl.ds(shard * per_shard, per_shard), rows_of]
        quarter = rows // 4
        return virt_all.at[pl.ds(pl.multiple_of(shard * rows + first * quarter, quarter), count * quarter)]

    def n_copy(which, way, q):
        first = 2 * core + q
        if which:
            quarter = width // 4
            src = occ.at[:, pl.ds(pl.multiple_of(first * quarter, quarter), quarter)]
        else:
            quarter = rows // 4
            src = virt.at[pl.ds(pl.multiple_of(first * quarter, quarter), quarter)]
        return pltpu.make_async_remote_copy(
            src_ref=src,
            dst_ref=piece(which, aux, first, 1),
            send_sem=n_send.at[which, way, q],
            recv_sem=n_recv.at[which, way, q],
            device_id={"aux": (beside, across)[way]},
            device_id_type=MESH,
        )

    def d_copy(which, q):
        place = piece(which, (beside, across)[q], 2 * core + q, 1)
        return pltpu.make_async_remote_copy(
            src_ref=place,
            dst_ref=place,
            send_sem=d_send.at[which, q],
            recv_sem=d_recv.at[which, q],
            device_id={"aux": (across, beside)[q]},
            device_id_type=MESH,
        )

    def s_copy(which, j):
        place = piece(which, (beside, across, corner)[j], 2 * core, 2)
        return pltpu.make_async_remote_copy(
            src_ref=place,
            dst_ref=place,
            send_sem=s_send.at[which, j],
            recv_sem=s_recv.at[which, j],
            device_id={"occ": sibling},
            device_id_type=MESH,
        )

    def f_copy(j):
        to = away(j)
        return pltpu.make_async_remote_copy(
            src_ref=fold.at[to],
            dst_ref=out.at[pl.ds(me * own, own)],
            send_sem=f_send.at[j - 1],
            recv_sem=f_recv.at[j - 1],
            device_id={"occ": to},
            device_id_type=MESH,
        )

    def each(action):
        def step(t, carry):
            action(half_group + (t + 1) // 2 * (2 * lax.rem(t, 2) - 1))
            return carry

        lax.fori_loop(0, peers - 1, step, 0)

    def spread(which):
        for late in range(2):
            for way in range(2):
                n_copy(which, way, (way + late) % 2).start()

    def pass_on(which):
        for way in range(2):
            n_copy(which, way, way).wait_recv()
            d_copy(which, way).start()

    def share_sides(which):
        for way in range(2):
            n_copy(which, way, 1 - way).wait_recv()
            s_copy(which, way).start()

    def share_corner(which):
        for q in range(2):
            d_copy(which, q).wait_recv()
        s_copy(which, 2).start()

    spread(0)
    each(lambda j: x_copy(j).start())
    for line, values in enumerate(slot_table(screening, pair_owner, half.shape[1], lines.shape[1])):
        lines[line : line + 1, :] = values
    for line in range(3, lines.shape[0]):
        lines[line : line + 1, :] = jnp.zeros_like(values)
    to_scalars = pltpu.make_async_copy(lines, table, local.at[4])
    to_scalars.start()
    pass_on(0)
    spread(1)
    share_sides(0)
    share_corner(0)
    pass_on(1)
    share_sides(1)
    for copy in keep:
        copy.wait()
    for j in range(3):
        s_copy(0, j).wait_recv()

    base = me // half_group * half_group

    def arrived(source):
        x_copy(lax.rem(me - source + peers, peers)).wait_recv()

    def project(p, start):
        def step(g, carry):
            x = moved[pl.ds(start, half_group), p]
            if inner % 16:
                x = x.astype(jnp.float32)
            count = half_group * inner
            x = x.reshape(count, x.shape[-1]).astype(jnp.bfloat16)
            v = virt_all[pl.ds(pl.multiple_of(g * rows, rows), rows), :]
            h = lax.dot_general(
                x, v, (((1,), (1,)), ((), ())), preferred_element_type=jnp.float32
            ).astype(jnp.bfloat16)
            place = pl.ds(pl.multiple_of(start * inner, count), count)
            for t in range(per_shard):
                half[p, g * per_shard + t, place, :] = h[:, t * width : (t + 1) * width]
            return carry

        lax.fori_loop(0, groups, step, 0)

    def near(t, carry):
        arrived(base + lax.rem(me - base + t, half_group))
        return carry

    def far(t, carry):
        arrived(half_group - base + t)
        return carry

    lax.fori_loop(1, half_group, near, 0)
    for p in range(own):
        project(p, base)
    share_corner(1)
    lax.fori_loop(0, half_group, far, 0)
    for p in range(own):
        project(p, half_group - base)

    for j in range(3):
        s_copy(1, j).wait_recv()
    to_scalars.wait()

    def block(p, r, c):
        return (
            jnp.dot(occ_all[r], half[p, c], preferred_element_type=jnp.float32)
            .astype(jnp.bfloat16)
            .astype(jnp.float32)
        )

    def make(j):
        to = away(j)
        for p in range(own):
            for s in range(MAXP):
                r = table[0, to * MAXP + s]
                c = table[1, to * MAXP + s]
                filled = table[2, to * MAXP + s].astype(jnp.float32)
                both = (block(p, r, c) + block(p, c, r).T) * filled
                fold[to, p, s] = both.astype(jnp.bfloat16)

    def finish(j):
        make(j)
        f_copy(j).start()

    each(finish)
    make(0)
    mine = pltpu.make_async_copy(fold.at[me], out.at[pl.ds(me * own, own)], local.at[3])
    mine.start()

    for which in range(2):
        for way in range(2):
            for q in range(2):
                n_copy(which, way, q).wait_send()
            d_copy(which, way).wait_send()
        for j in range(3):
            s_copy(which, j).wait_send()
    each(lambda j: x_copy(j).wait_send())
    each(lambda j: f_copy(j).wait_recv())
    each(lambda j: f_copy(j).wait_send())
    mine.wait()


def per_device(groups, peers, amplitudes, virtual_orbitals, occupied_orbitals, screening, pair_owner, pair_weight):
    group_size, inner, virtual_count = amplitudes.shape
    rows = virtual_orbitals.shape[0]
    occupied_count = occupied_orbitals.shape[1]
    own = group_size // peers
    nblocks = screening.shape[0]
    width = pair_weight.shape[1]
    lanes = -(-peers * MAXP // 128) * 128
    kind = jnp.bfloat16
    dma = pltpu.SemaphoreType.DMA
    folded = pl.pallas_call(
        functools.partial(fused, groups, peers),
        out_shape=jax.ShapeDtypeStruct((group_size, MAXP, width, width), kind),
        in_specs=[pl.BlockSpec(memory_space=pltpu.SMEM)] * 2 + [pl.BlockSpec(memory_space=pl.ANY)] * 3,
        out_specs=pl.BlockSpec(memory_space=pl.ANY),
        scratch_shapes=[
            pltpu.VMEM((peers, own, inner, virtual_count), kind),
            pltpu.VMEM((groups * rows, virtual_count), kind),
            pltpu.VMEM((nblocks, width, occupied_count), kind),
            pltpu.VMEM((own, nblocks, occupied_count, width), kind),
            pltpu.VMEM((peers, own, MAXP, width, width), kind),
            pltpu.VMEM((8, lanes), jnp.int32),
            pltpu.SMEM((8, lanes), jnp.int32),
            dma((peers - 1,)),
            dma((peers - 1,)),
            dma((2, 2, 2)),
            dma((2, 2, 2)),
            dma((2, 2)),
            dma((2, 2)),
            dma((2, 3)),
            dma((2, 3)),
            dma((peers - 1,)),
            dma((peers - 1,)),
            dma((5,)),
        ],
        compiler_params=pltpu.CompilerParams(
            collective_id=0, has_side_effects=True, vmem_limit_bytes=60 * 1024 * 1024
        ),
    )(
        screening,
        pair_owner,
        amplitudes,
        virtual_orbitals,
        occupied_orbitals.reshape(rows // width, width, occupied_count),
    )
    weights = pair_weight.astype(jnp.float32)[None]
    return (weights * folded.astype(jnp.float32)).astype(jnp.bfloat16)


def solution(mesh):
    return jax.shard_map(
        functools.partial(per_device, mesh.shape["aux"], mesh.shape["occ"]),
        mesh=mesh,
        in_specs=(
            P("aux", "occ", None),
            P("aux", None),
            P("aux", None),
            P(),
            P(),
            P("occ", None, None),
        ),
        out_specs=P("aux", "occ", None, None),
        check_vma=False,
    )
```

```python
import functools

import jax
import jax.numpy as jnp
from jax import lax
from jax.experimental import pallas as pl
from jax.experimental.pallas import tpu as pltpu
from jax.sharding import PartitionSpec as P

MAXP = 2
MESH = pl.DeviceIdType.MESH


def slot_table(screening, pair_owner, nblocks, lanes):
    lane = lax.broadcasted_iota(jnp.int32, (1, lanes), 1)
    owner, rank = lane // MAXP, lane % MAXP

    def row(r, carry):
        def column(c, carry):
            rows, columns, filled, count = carry
            kept = (owner == pair_owner[r, c]) & (jnp.full_like(lane, screening[r, c]) == 1)
            here = kept & (rank == count)
            return (
                jnp.where(here, r, rows),
                jnp.where(here, c, columns),
                jnp.where(here, 1, filled),
                jnp.where(kept, count + 1, count),
            )

        return lax.fori_loop(r, nblocks, column, carry)

    none = jnp.zeros_like(lane)
    return lax.fori_loop(0, nblocks, row, (none,) * 4)[:3]


def fused(
    groups, peers,
    screening, pair_owner, amp, virt, occ, out,
    moved, virt_all, occ_all, half, fold, lines, table,
    x_send, x_recv, n_send, n_recv, d_send, d_recv, s_send, s_recv, f_send, f_recv, local,
):
    aux = lax.axis_index("aux")
    me = lax.axis_index("occ")
    core = lax.rem(me, 2)
    sibling = me + 1 - 2 * core
    own = moved.shape[1]
    inner = moved.shape[2]
    rows = virt.shape[0]
    half_group = peers // 2
    width = half.shape[3]
    per_shard = rows // width

    def away(j):
        return lax.rem(me + j, peers)

    beside = aux + 1 - 2 * lax.rem(aux, 2)
    across = lax.rem(aux + 2, groups)
    corner = lax.rem(beside + 2, groups)

    barrier = pltpu.get_barrier_semaphore()

    def greet(j, carry):
        pl.semaphore_signal(barrier, inc=1, device_id={"occ": away(j)}, device_id_type=MESH)
        return carry

    lax.fori_loop(1, peers, greet, 0)
    for near in (beside, across):
        pl.semaphore_signal(barrier, inc=1, device_id={"aux": near}, device_id_type=MESH)

    keep = [
        pltpu.make_async_copy(virt, virt_all.at[pl.ds(pl.multiple_of(aux * rows, rows), rows)], local.at[0]),
        pltpu.make_async_copy(occ, occ_all.at[pl.ds(aux * per_shard, per_shard)], local.at[1]),
        pltpu.make_async_copy(amp.at[pl.ds(me * own, own)], moved.at[me], local.at[2]),
    ]
    for copy in keep:
        copy.start()
    for line, values in enumerate(slot_table(screening, pair_owner, half.shape[1], lines.shape[1])):
        lines[line : line + 1, :] = values
    for line in range(3, lines.shape[0]):
        lines[line : line + 1, :] = jnp.zeros_like(values)
    to_scalars = pltpu.make_async_copy(lines, table, local.at[4])
    to_scalars.start()
    pl.semaphore_wait(barrier, peers + 1)

    def x_copy(j):
        to = away(j)
        return pltpu.make_async_remote_copy(
            src_ref=amp.at[pl.ds(to * own, own)],
            dst_ref=moved.at[me],
            send_sem=x_send.at[j - 1],
            recv_sem=x_recv.at[j - 1],
            device_id={"occ": to},
            device_id_type=MESH,
        )

    def piece(which, shard, first, count):
        if which:
            quarter = width // 4
            rows_of = pl.ds(pl.multiple_of(first * quarter, quarter), count * quarter)
            return occ_all.at[pl.ds(shard * per_shard, per_shard), rows_of]
        quarter = rows // 4
        return virt_all.at[pl.ds(pl.multiple_of(shard * rows + first * quarter, quarter), count * quarter)]

    def n_copy(which, way, q):
        first = 2 * core + q
        if which:
            quarter = width // 4
            src = occ.at[:, pl.ds(pl.multiple_of(first * quarter, quarter), quarter)]
        else:
            quarter = rows // 4
            src = virt.at[pl.ds(pl.multiple_of(first * quarter, quarter), quarter)]
        return pltpu.make_async_remote_copy(
            src_ref=src,
            dst_ref=piece(which, aux, first, 1),
            send_sem=n_send.at[which, way, q],
            recv_sem=n_recv.at[which, way, q],
            device_id={"aux": (beside, across)[way]},
            device_id_type=MESH,
        )

    def d_copy(which, q):
        place = piece(which, (beside, across)[q], 2 * core + q, 1)
        return pltpu.make_async_remote_copy(
            src_ref=place,
            dst_ref=place,
            send_sem=d_send.at[which, q],
            recv_sem=d_recv.at[which, q],
            device_id={"aux": (across, beside)[q]},
            device_id_type=MESH,
        )

    def s_copy(which, j):
        place = piece(which, (beside, across, corner)[j], 2 * core, 2)
        return pltpu.make_async_remote_copy(
            src_ref=place,
            dst_ref=place,
            send_sem=s_send.at[which, j],
            recv_sem=s_recv.at[which, j],
            device_id={"occ": sibling},
            device_id_type=MESH,
        )

    def f_copy(j):
        to = away(j)
        return pltpu.make_async_remote_copy(
            src_ref=fold.at[to],
            dst_ref=out.at[pl.ds(me * own, own)],
            send_sem=f_send.at[j - 1],
            recv_sem=f_recv.at[j - 1],
            device_id={"occ": to},
            device_id_type=MESH,
        )

    def each(action):
        def step(t, carry):
            action(half_group + (t + 1) // 2 * (2 * lax.rem(t, 2) - 1))
            return carry

        lax.fori_loop(0, peers - 1, step, 0)

    def spread(which):
        for late in range(2):
            for way in range(2):
                n_copy(which, way, (way + late) % 2).start()

    def pass_on(which):
        for way in range(2):
            n_copy(which, way, way).wait_recv()
            d_copy(which, way).start()

    def share_sides(which):
        for way in range(2):
            n_copy(which, way, 1 - way).wait_recv()
            s_copy(which, way).start()

    def share_corner(which):
        for q in range(2):
            d_copy(which, q).wait_recv()
        s_copy(which, 2).start()

    spread(0)
    each(lambda j: x_copy(j).start())
    pass_on(0)
    spread(1)
    share_sides(0)
    share_corner(0)
    pass_on(1)
    share_sides(1)
    for copy in keep:
        copy.wait()
    for j in range(3):
        s_copy(0, j).wait_recv()

    base = me // half_group * half_group

    def arrived(source):
        x_copy(lax.rem(me - source + peers, peers)).wait_recv()

    def project(p, start):
        def step(g, carry):
            x = moved[pl.ds(start, half_group), p]
            if inner % 16:
                x = x.astype(jnp.float32)
            count = half_group * inner
            x = x.reshape(count, x.shape[-1]).astype(jnp.bfloat16)
            v = virt_all[pl.ds(pl.multiple_of(g * rows, rows), rows), :]
            h = lax.dot_general(
                x, v, (((1,), (1,)), ((), ())), preferred_element_type=jnp.float32
            ).astype(jnp.bfloat16)
            place = pl.ds(pl.multiple_of(start * inner, count), count)
            for t in range(per_shard):
                half[p, g * per_shard + t, place, :] = h[:, t * width : (t + 1) * width]
            return carry

        lax.fori_loop(0, groups, step, 0)

    def near(t, carry):
        arrived(base + lax.rem(me - base + t, half_group))
        return carry

    def far(t, carry):
        arrived(half_group - base + t)
        return carry

    lax.fori_loop(1, half_group, near, 0)
    for p in range(own):
        project(p, base)
    share_corner(1)
    lax.fori_loop(0, half_group, far, 0)
    for p in range(own):
        project(p, half_group - base)

    for j in range(3):
        s_copy(1, j).wait_recv()
    to_scalars.wait()

    def block(p, r, c):
        return (
            jnp.dot(occ_all[r], half[p, c], preferred_element_type=jnp.float32)
            .astype(jnp.bfloat16)
            .astype(jnp.float32)
        )

    def make(j):
        to = away(j)
        for p in range(own):
            for s in range(MAXP):
                r = table[0, to * MAXP + s]
                c = table[1, to * MAXP + s]
                filled = table[2, to * MAXP + s].astype(jnp.float32)
                both = (block(p, r, c) + block(p, c, r).T) * filled
                fold[to, p, s] = both.astype(jnp.bfloat16)

    def finish(j):
        make(j)
        f_copy(j).start()

    each(finish)
    make(0)
    mine = pltpu.make_async_copy(fold.at[me], out.at[pl.ds(me * own, own)], local.at[3])
    mine.start()

    for which in range(2):
        for way in range(2):
            for q in range(2):
                n_copy(which, way, q).wait_send()
            d_copy(which, way).wait_send()
        for j in range(3):
            s_copy(which, j).wait_send()
    each(lambda j: x_copy(j).wait_send())
    each(lambda j: f_copy(j).wait_recv())
    each(lambda j: f_copy(j).wait_send())
    mine.wait()


def per_device(groups, peers, amplitudes, virtual_orbitals, occupied_orbitals, screening, pair_owner, pair_weight):
    group_size, inner, virtual_count = amplitudes.shape
    rows = virtual_orbitals.shape[0]
    occupied_count = occupied_orbitals.shape[1]
    own = group_size // peers
    nblocks = screening.shape[0]
    width = pair_weight.shape[1]
    lanes = -(-peers * MAXP // 128) * 128
    kind = jnp.bfloat16
    dma = pltpu.SemaphoreType.DMA
    folded = pl.pallas_call(
        functools.partial(fused, groups, peers),
        out_shape=jax.ShapeDtypeStruct((group_size, MAXP, width, width), kind),
        in_specs=[pl.BlockSpec(memory_space=pltpu.SMEM)] * 2 + [pl.BlockSpec(memory_space=pl.ANY)] * 3,
        out_specs=pl.BlockSpec(memory_space=pl.ANY),
        scratch_shapes=[
            pltpu.VMEM((peers, own, inner, virtual_count), kind),
            pltpu.VMEM((groups * rows, virtual_count), kind),
            pltpu.VMEM((nblocks, width, occupied_count), kind),
            pltpu.VMEM((own, nblocks, occupied_count, width), kind),
            pltpu.VMEM((peers, own, MAXP, width, width), kind),
            pltpu.VMEM((8, lanes), jnp.int32),
            pltpu.SMEM((8, lanes), jnp.int32),
            dma((peers - 1,)),
            dma((peers - 1,)),
            dma((2, 2, 2)),
            dma((2, 2, 2)),
            dma((2, 2)),
            dma((2, 2)),
            dma((2, 3)),
            dma((2, 3)),
            dma((peers - 1,)),
            dma((peers - 1,)),
            dma((5,)),
        ],
        compiler_params=pltpu.CompilerParams(
            collective_id=0, has_side_effects=True, vmem_limit_bytes=60 * 1024 * 1024
        ),
    )(
        screening,
        pair_owner,
        amplitudes,
        virtual_orbitals,
        occupied_orbitals.reshape(rows // width, width, occupied_count),
    )
    weights = pair_weight.astype(jnp.float32)[None]
    return (weights * folded.astype(jnp.float32)).astype(jnp.bfloat16)


def solution(mesh):
    return jax.shard_map(
        functools.partial(per_device, mesh.shape["aux"], mesh.shape["occ"]),
        mesh=mesh,
        in_specs=(
            P("aux", "occ", None),
            P("aux", None),
            P("aux", None),
            P(),
            P(),
            P("occ", None, None),
        ),
        out_specs=P("aux", "occ", None, None),
        check_vma=False,
    )
```
